32 devices in a mesh: seq: 8 (over y, x, core), head: 4 (over z).
Axes of the slice: x: 2, y: 2, z: 4, core: 2. Of those that a mesh axis runs over, the one named last changes fastest.
Arguments:
- tokens: bfloat16 [8192, 2048], P('seq'), may hold values from -6 to 6
- norm_gain: float32 [1, 2, 2048], replicated, may hold values from 0.1 to 1.9
- norm_bias: float32 [1, 2, 2048], replicated, may hold values from -1.5 to 1.5
- query_weight: bfloat16 [1, 2048, 2048], P(None, None, 'head'), may hold values from -0.125 to 0.125
- key_weight: bfloat16 [1, 2048, 2048], P(None, None, 'head'), may hold values from -0.125 to 0.125
- value_weight: bfloat16 [1, 2048, 3456], P(None, None, 'head'), may hold values from -0.125 to 0.125
- gate_weight: bfloat16 [1, 2048, 3456], P(None, None, 'head'), may hold values from -0.125 to 0.125
- output_weight: bfloat16 [1, 3456, 2048], P(None, 'head'), may hold values from -0.15625 to 0.15625
- ffn_gate: bfloat16 [1, 2048, 3456], P(None, None, 'head'), may hold values from -0.125 to 0.125
- ffn_up: bfloat16 [1, 2048, 3456], P(None, None, 'head'), may hold values from -0.125 to 0.125
- ffn_down: bfloat16 [1, 3456, 2048], P(None, 'head'), may hold values from -0.15625 to 0.15625
- grad_out: bfloat16 [8192, 2048], P('seq'), may hold values from -6 to 6
Outputs:
- result: bfloat16 [8192, 2048], P('seq')
- grad_tokens: float32 [8192, 2048], P('seq')
- grad_norm_gain: float32 [1, 2, 2048], P(None, None, 'seq')
- grad_norm_bias: float32 [1, 2, 2048], P(None, None, 'seq')
- grad_query_weight: float32 [1, 2048, 2048], P(None, 'seq', 'head')
- grad_key_weight: float32 [1, 2048, 2048], P(None, 'seq', 'head')
- grad_value_weight: float32 [1, 2048, 3456], P(None, 'seq', 'head')
- grad_gate_weight: float32 [1, 2048, 3456], P(None, 'seq', 'head')
- grad_output_weight: float32 [1, 3456, 2048], P(None, 'head', 'seq')
- grad_ffn_gate: float32 [1, 2048, 3456], P(None, 'seq', 'head')
- grad_ffn_up: float32 [1, 2048, 3456], P(None, 'seq', 'head')
- grad_ffn_down: float32 [1, 3456, 2048], P(None, 'head', 'seq')
The draws below stay inside these ranges and needn't reach their ends.
All inputs are finite; a program needn't handle non-finite values.
Results may differ from the reference program's by a relative error of at most 0.025.
Values may be sent and summed in bfloat16 or wider, within the bound.
No kernel may reach another device: no remote copies, remote signals or barrier semaphores. Data moves between devices by JAX's collectives and lax.ppermute only.
A program may use at most 256 MiB of HBM per device.

```python
import jax
import jax.numpy as jnp
from jax import lax

D = 2048
HEADS = 8
KEY_DIM = 256
VAL_DIM = 432
FF = 3456
LAYERS = 1
TOK_DEV = 1024
TOKENS = 8192
N_SEQ = 8
N_HEAD = 4


def block_levels(own_key, dims, cuts, least, top_value):
    def one(position, parts):
        heights = jax.random.uniform(jax.random.fold_in(jax.random.fold_in(own_key, 6), position), (parts,), jnp.float32, least / len(cuts), top_value / len(cuts))
        return jnp.repeat(jnp.exp(heights), dims[position] // parts).reshape((-1,) + (1,) * (len(dims) - position - 1))

    level = one(*cuts[0])
    for cut in cuts[1:]:
        level = level * one(*cut)
    return level


def scatter_about(own_key, shape, deviation, reach, split=(), held_as=jnp.bfloat16):
    factor_of = block_levels(own_key, shape, split, -0.22, 0.18) if split else 1.0
    drawn = jax.random.normal(own_key, shape, jnp.float32) * deviation * factor_of
    return jnp.minimum(jnp.maximum(drawn, -reach), reach).astype(held_as)


def setup_inputs(seed: int = 0) -> dict:
    key_list = jax.random.split(jax.random.key(seed), 13)
    tokens = scatter_about(key_list[0], (TOKENS, D), 1.0, 6.0, ((0, 8),))
    norm_gain = jnp.clip(1.0 + 0.18 * jax.random.normal(key_list[1], (LAYERS, 2, D), jnp.float32), 0.1, 1.9)
    norm_bias = scatter_about(key_list[2], (LAYERS, 2, D), 0.3, 1.5, (), jnp.float32)
    query_weight = scatter_about(key_list[3], (LAYERS, D, D), D ** -0.5, 0.125, ((2, 4),))
    key_weight = scatter_about(key_list[4], (LAYERS, D, D), D ** -0.5, 0.125, ((2, 4),))
    value_weight = scatter_about(key_list[5], (LAYERS, D, HEADS * VAL_DIM), D ** -0.5, 0.125, ((2, 4),))
    gate_weight = scatter_about(key_list[6], (LAYERS, D, HEADS * VAL_DIM), D ** -0.5, 0.125, ((2, 4),))
    output_weight = scatter_about(key_list[7], (LAYERS, HEADS * VAL_DIM, D), (HEADS * VAL_DIM // 2) ** -0.5, 0.15625, ((1, 4),))
    ffn_gate = scatter_about(key_list[8], (LAYERS, D, FF), D ** -0.5, 0.125, ((2, 4),))
    ffn_up = scatter_about(key_list[9], (LAYERS, D, FF), D ** -0.5, 0.125, ((2, 4),))
    ffn_down = scatter_about(key_list[10], (LAYERS, FF, D), (FF // 2) ** -0.5, 0.15625, ((1, 4),))
    grad_out = scatter_about(key_list[11], (TOKENS, D), 1.0, 6.0, ((0, 8),))
    return {"tokens": tokens, "norm_gain": norm_gain, "norm_bias": norm_bias, "query_weight": query_weight, "key_weight": key_weight, "value_weight": value_weight, "gate_weight": gate_weight, "output_weight": output_weight, "ffn_gate": ffn_gate, "ffn_up": ffn_up, "ffn_down": ffn_down, "grad_out": grad_out}


@jax.custom_vjp
def low(v):
    return lax.optimization_barrier(v.astype(jnp.bfloat16)).astype(jnp.float32)

@jax.custom_vjp
def low_back(v):
    return v

def low_keep(v):
    return (low(v), None)

def low_pass(kept, grad):
    return (grad,)

def back_keep(v):
    return (v, None)

def back_low(kept, grad):
    return (low(grad),)
low.defvjp(low_keep, low_pass)
low_back.defvjp(back_keep, back_low)
EPS = 1e-05

def mult(left, right):
    return jnp.dot(left, right, precision=lax.Precision.HIGHEST, preferred_element_type=jnp.float32)

def layer_norm(values, gain, bias):
    mean = lax.optimization_barrier(jnp.mean(values, axis=-1, keepdims=True))
    centred = values - mean
    spread = lax.optimization_barrier(jnp.mean(centred * centred, axis=-1, keepdims=True))
    return centred * lax.rsqrt(spread + EPS) * gain + bias

def group_norm(values):
    mean = lax.optimization_barrier(jnp.mean(values, axis=-1, keepdims=True))
    centred = values - mean
    spread = lax.optimization_barrier(jnp.mean(centred * centred, axis=-1, keepdims=True))
    return centred * lax.rsqrt(spread + EPS)

def rotate(values, positions):
    half = KEY_DIM // 2
    freqs = 1.0 / 10000.0 ** jnp.linspace(0.0, 1.0, half, dtype=jnp.float32)
    angles = positions[:, None] * freqs[None, :]
    cosine = jnp.cos(angles)[:, None, :]
    sine = jnp.sin(angles)[:, None, :]
    shaped = values.reshape(values.shape[0], -1, KEY_DIM)
    first = shaped[..., :half]
    second = shaped[..., half:]
    turned = jnp.concatenate([first * cosine - second * sine, second * cosine + first * sine], axis=-1)
    return turned.reshape(values.shape)

def split_sum(left, right):
    width = left.shape[1] // N_HEAD
    total = jnp.zeros((left.shape[0], right.shape[1]), jnp.float32)
    for group in range(N_HEAD):
        total = total + low(mult(left[:, group * width:(group + 1) * width], right[group * width:(group + 1) * width]))
    return total

def retain(queries, keys, values):
    log_decay = jnp.log1p(-jnp.exp2(-5.0 - jnp.arange(HEADS, dtype=jnp.float32)))
    offsets = jnp.arange(TOK_DEV, dtype=jnp.float32)
    diff = offsets[:, None] - offsets[None, :]
    causal = diff >= 0
    within = jnp.where(causal[None], jnp.exp(jnp.where(causal, diff, 0.0)[None] * log_decay[:, None, None]), 0.0)
    query_decay = jnp.exp((offsets + 1.0)[:, None] * log_decay[None, :])
    key_decay = jnp.exp((TOK_DEV - 1.0 - offsets)[:, None] * log_decay[None, :])
    block_decay = jnp.exp(TOK_DEV * log_decay)

    def block_step(running_state, pieces):
        query_block, key_block, value_tile_block = pieces
        scores = low_back(jnp.einsum('thk,shk->hts', query_block, key_block, precision=lax.Precision.HIGHEST))
        weights = low(scores * within)
        query_rescaled = low(query_block * query_decay[:, :, None])
        key_rescaled = low(key_block * key_decay[:, :, None])
        layer_output = jnp.einsum('hts,shv->thv', weights, value_tile_block, precision=lax.Precision.HIGHEST)
        layer_output = layer_output + jnp.einsum('gsc,scr->gsr', query_rescaled, low(running_state), precision=lax.Precision.HIGHEST)
        layer_output = low_back(layer_output)
        segment_state = low_back(jnp.einsum('ufb,ufn->fbn', key_rescaled, value_tile_block, precision=lax.Precision.HIGHEST))
        return (running_state * block_decay[:, None, None] + segment_state, layer_output)
    start = jnp.zeros((HEADS, KEY_DIM, VAL_DIM), jnp.float32)
    blocks = (queries.reshape(N_SEQ, TOK_DEV, HEADS, KEY_DIM), keys.reshape(N_SEQ, TOK_DEV, HEADS, KEY_DIM), values.reshape(N_SEQ, TOK_DEV, HEADS, VAL_DIM))
    final_state, outputs = lax.scan(jax.checkpoint(block_step), start, blocks)
    return outputs.reshape(TOKENS, HEADS, VAL_DIM)

def one_layer(inputs, gains, biases, query_w, key_w, value_w, gate_w, output_w, ffn_gate_w, ffn_up_w, ffn_down_w, positions):
    normed = low(layer_norm(inputs, gains[0], biases[0]))
    query_raw = low_back(mult(normed, query_w))
    key_raw = low_back(mult(normed, key_w))
    values = low(low_back(mult(normed, value_w)))
    gate_raw = low_back(mult(normed, gate_w))
    queries = low(rotate(query_raw, positions) / jnp.sqrt(jnp.float32(KEY_DIM)))
    keys = low(rotate(key_raw, positions))
    retained = retain(queries.reshape(TOKENS, HEADS, KEY_DIM), keys.reshape(TOKENS, HEADS, KEY_DIM), values.reshape(TOKENS, HEADS, VAL_DIM))
    gated = low(jax.nn.silu(gate_raw) * group_norm(retained).reshape(TOKENS, HEADS * VAL_DIM))
    middle = inputs + low_back(split_sum(gated, output_w))
    ffn_in = low(layer_norm(middle, gains[1], biases[1]))
    gate_pre = low_back(mult(ffn_in, ffn_gate_w))
    up_pre = low_back(mult(ffn_in, ffn_up_w))
    hidden = low(jax.nn.gelu(gate_pre) * up_pre)
    return middle + low_back(split_sum(hidden, ffn_down_w))

def forward(inputs, norm_gain, norm_bias, query_weight, key_weight, value_weight, gate_weight, output_weight, ffn_gate, ffn_up, ffn_down):
    positions = jnp.arange(TOKENS, dtype=jnp.float32)
    for layer_index in range(LAYERS):
        inputs = one_layer(inputs, norm_gain[layer_index], norm_bias[layer_index], query_weight[layer_index], key_weight[layer_index], value_weight[layer_index], gate_weight[layer_index], output_weight[layer_index], ffn_gate[layer_index], ffn_up[layer_index], ffn_down[layer_index], positions)
    return inputs

def reference(tokens, norm_gain, norm_bias, query_weight, key_weight, value_weight, gate_weight, output_weight, ffn_gate, ffn_up, ffn_down, grad_out):
    params = (tokens.astype(jnp.float32), norm_gain.astype(jnp.float32), norm_bias.astype(jnp.float32), query_weight.astype(jnp.float32), key_weight.astype(jnp.float32), value_weight.astype(jnp.float32), gate_weight.astype(jnp.float32), output_weight.astype(jnp.float32), ffn_gate.astype(jnp.float32), ffn_up.astype(jnp.float32), ffn_down.astype(jnp.float32))
    outcome, pull = jax.vjp(forward, *params)
    grads = pull(grad_out.astype(jnp.float32))
    return (outcome.astype(jnp.bfloat16), grads[0], grads[1], grads[2], grads[3], grads[4], grads[5], grads[6], grads[7], grads[8], grads[9], grads[10])
```

```python
import jax
import jax.numpy as jnp
from jax import lax
from jax.experimental import pallas as pl
from jax.experimental.pallas import tpu as pltpu
from jax.sharding import PartitionSpec as P

KEY_DIM = 256
VAL_DIM = 432
EPS = 1e-05
CHUNKS = 4


def matmul(left, right):
    return jnp.dot(left, right, preferred_element_type=jnp.float32)


def matmul_left(left, right):
    return lax.dot_general(
        left, right, (((0,), (0,)), ((), ())), preferred_element_type=jnp.float32
    )


def matmul_right(left, right):
    return lax.dot_general(
        left, right, (((1,), (1,)), ((), ())), preferred_element_type=jnp.float32
    )


def low(values):
    return values.astype(jnp.bfloat16)


def wide(values):
    return values.astype(jnp.float32)


ANY = pl.BlockSpec(memory_space=pl.ANY)
SMEM = pl.BlockSpec(memory_space=pltpu.SMEM)
VMEM = pl.BlockSpec(memory_space=pltpu.VMEM)
EXTRA_ROWS = 32


def params(mebibytes):
    return pltpu.CompilerParams(vmem_limit_bytes=mebibytes * 2**20)


def small_cost():
    return pl.CostEstimate(flops=0, bytes_accessed=1_000_000, transcendentals=0)


def struct(shape, dtype):
    return jax.ShapeDtypeStruct(tuple(shape), dtype)


def in_hbm(shape, dtype=jnp.bfloat16):
    return pltpu.HBM(tuple(shape), dtype)


def pin(values):
    return pltpu.with_memory_space_constraint(values, pltpu.HBM)


def vmem(shape, dtype=jnp.bfloat16):
    return pltpu.VMEM(tuple(shape), dtype)


def fetch(source, target, sem):
    copy = pltpu.make_async_copy(source, target, sem)
    copy.start()
    return copy


def tiles(rows, body, size=256):
    for start in range(0, rows, size):
        body(pl.ds(start, min(size, rows - start)))


def row_mean(values):
    return jnp.mean(values, axis=-1, keepdims=True)


def norm_back(grad, unit, scale):
    return scale * (grad - row_mean(grad) - unit * row_mean(grad * unit))


def norm_parts(values):
    mean = row_mean(values)
    centred = values - mean
    scale = lax.rsqrt(row_mean(centred * centred) + EPS)
    return centred * scale, mean, scale


def spread_lanes(column):
    return jnp.broadcast_to(column, (column.shape[0], 128))


def turn(values, cosine, sine):
    half = KEY_DIM // 2
    parts = []
    for start in range(0, values.shape[1], KEY_DIM):
        first = values[:, start : start + half]
        second = values[:, start + half : start + KEY_DIM]
        parts += [first * cosine - second * sine, second * cosine + first * sine]
    return jnp.concatenate(parts, axis=1)


def decay_rows(log_decay, first, rows, sign):
    row = lax.broadcasted_iota(jnp.int32, (rows, KEY_DIM), 0).astype(jnp.float32)
    return jnp.exp((first + sign * row) * log_decay)


def decay_square(log_decay, apart, size):
    t = lax.broadcasted_iota(jnp.int32, (size, size), 0)
    s = lax.broadcasted_iota(jnp.int32, (size, size), 1)
    gap = apart + t - s
    table = jnp.exp(jnp.maximum(gap, 0).astype(jnp.float32) * log_decay)
    return jnp.where(gap >= 0, table, 0.0) if apart == 0 else table


def add_call(held, came):
    rows, cols = held.shape

    def kernel(held, came, out):
        out[...] = (wide(held[...]) + wide(came[...])).astype(out.dtype)

    spec = pl.BlockSpec((rows // 2, cols), lambda i: (i, 0))
    return pl.pallas_call(
        kernel,
        grid=(2,),
        in_specs=[spec, spec],
        out_specs=spec,
        out_shape=struct(held.shape, held.dtype),
        compiler_params=params(8),
        cost_estimate=small_cost(),
    )(held, came)


def first_call(decay, tok, gain, bias, cos, sin, key_w, value_w):
    rows, width = tok.shape
    keys, values = key_w.shape[1], value_w.shape[0]
    heads = keys // KEY_DIM
    size = rows // CHUNKS

    def kernel(decay, tok, gain, bias, cos, sin, key_w, value_w, normed, mean_out, scale_out, key, value, state, tok_v, key_v, value_v, normed_v, product, sems):
        span = lambda i: pl.ds(i * size, size)
        loads = [fetch(tok.at[span(i)], tok_v.at[span(i)], sems.at[i]) for i in range(CHUNKS)]
        load_key = fetch(key_w, key_v, sems.at[CHUNKS])
        load_value = fetch(value_w, value_v, sems.at[CHUNKS + 1])
        stores = []
        for i in range(CHUNKS):
            loads[i].wait()

            def norm(part):
                unit, mean, scale = norm_parts(wide(tok_v[part]))
                normed_v[part] = low(unit * gain[0:1] + bias[0:1])
                mean_out[part] = spread_lanes(mean)
                scale_out[part] = spread_lanes(scale)

            norm(span(i))
            stores.append(fetch(normed_v.at[span(i)], normed.at[span(i)], sems.at[CHUNKS + 2 + i]))
        load_key.wait()
        product[...] = matmul(normed_v[...], key_v[...])

        def rotate(part):
            key[part] = low(turn(product[part], cos[part], sin[part]))

        tiles(rows, rotate)
        load_value.wait()
        value[...] = low(matmul_right(value_v[...], normed_v[...]))
        for head in range(heads):
            k = wide(key[:, head * KEY_DIM : (head + 1) * KEY_DIM])
            scaled = low(k * decay_rows(decay[head], rows - 1.0, rows, -1.0))
            v = value[head * VAL_DIM : (head + 1) * VAL_DIM]
            state[head] = low(matmul(v, scaled))
        for store in stores:
            store.wait()

    return pl.pallas_call(
        kernel,
        in_specs=[SMEM, ANY, VMEM, VMEM, VMEM, VMEM, ANY, ANY],
        out_specs=[ANY] + [VMEM] * 5,
        out_shape=[
            in_hbm((rows, width)),
            in_hbm((rows, 128), jnp.float32),
            in_hbm((rows, 128), jnp.float32),
            in_hbm((rows, keys)),
            in_hbm((values, rows)),
            struct((heads, VAL_DIM, KEY_DIM), jnp.bfloat16),
        ],
        scratch_shapes=[
            vmem((rows, width)),
            vmem(key_w.shape),
            vmem(value_w.shape),
            vmem((rows, width)),
            vmem((rows, keys), jnp.float32),
            pltpu.SemaphoreType.DMA((2 * CHUNKS + 2,)),
        ],
        compiler_params=params(50),
        cost_estimate=small_cost(),
    )(decay, pin(tok), gain, bias, cos, sin, pin(key_w), pin(value_w))


def second_call(place, normed, cos, sin, query_w, gate_w):
    rows, width = normed.shape
    keys, values = query_w.shape[1], gate_w.shape[0]
    count = place.shape[0] - 1
    block = width // count

    def kernel(place, normed, cos, sin, query_w, gate_w, query, gate, arranged, normed_v, query_v, gate_v, product, sems):
        load = fetch(normed, normed_v, sems.at[0])
        load_query = fetch(query_w, query_v, sems.at[1])
        load_gate = fetch(gate_w, gate_v, sems.at[2])
        load.wait()
        stores = []
        for b in range(count):
            start = pl.multiple_of(place[1 + b] * block, block)
            source = normed_v.at[:, pl.ds(b * block, block)]
            stores.append(fetch(source, arranged.at[:, pl.ds(start, block)], sems.at[3 + b]))
        load_query.wait()
        product[...] = matmul(normed_v[...], query_v[...])

        def rotate(part):
            turned = turn(product[part], cos[part], sin[part])
            query[part] = low(turned * (1.0 / KEY_DIM**0.5))

        tiles(rows, rotate)
        load_gate.wait()
        gate[...] = low(matmul_right(gate_v[...], normed_v[...]))
        for store in stores:
            store.wait()

    return pl.pallas_call(
        kernel,
        in_specs=[SMEM, ANY, VMEM, VMEM, ANY, ANY],
        out_specs=[VMEM, VMEM, ANY],
        out_shape=[in_hbm((rows, keys)), in_hbm((values, rows)), in_hbm((rows, width))],
        scratch_shapes=[
            vmem((rows, width)),
            vmem(query_w.shape),
            vmem(gate_w.shape),
            vmem((rows, keys), jnp.float32),
            pltpu.SemaphoreType.DMA((3 + count,)),
        ],
        compiler_params=params(44),
        cost_estimate=small_cost(),
    )(place, pin(normed), cos, sin, pin(query_w), pin(gate_w))


def intra_call(decay, query, key, value):
    rows = query.shape[0]
    heads = query.shape[1] // KEY_DIM
    size = rows // CHUNKS

    def kernel(decay, query, key, value, intra):
        span = lambda i: slice(i * size, (i + 1) * size)
        rate = decay[pl.program_id(0)]
        tables = [decay_square(rate, d * size, size) for d in range(CHUNKS)]
        for i in range(CHUNKS):
            q = query[span(i)]
            weights = [
                low(matmul_right(q, key[span(j)]) * tables[i - j]) for j in range(i + 1)
            ]
            weights = jnp.concatenate(weights, axis=1) if i else weights[0]
            intra[:, span(i)] = matmul_right(value[:, : (i + 1) * size], weights)

    column = pl.BlockSpec((rows, KEY_DIM), lambda h: (0, h))
    per_head = pl.BlockSpec((VAL_DIM, rows), lambda h: (h, 0))
    return pl.pallas_call(
        kernel,
        grid=(heads,),
        in_specs=[SMEM, column, column, per_head],
        out_specs=per_head,
        out_shape=in_hbm((heads * VAL_DIM, rows), jnp.float32),
        compiler_params=params(44),
        cost_estimate=small_cost(),
    )(decay, pin(query), pin(key), pin(value))


def mix_call(index, decay, query, gate, intra, state, output_w, buffers):
    rows, keys = query.shape
    values, width = output_w.shape
    heads = keys // KEY_DIM
    size = rows // CHUNKS
    first = buffers is None

    def kernel(decay, query, gate, intra, state, output_w, *refs):
        refs = refs if first else refs[2:]
        part, scale_out, gated, units = refs[:4]
        query_v, gate_v, intra_v, weight, gated_v, unit_v, sems = refs[4:]
        here = pl.ds(index * size, size)
        loads = [
            fetch(query.at[here], query_v, sems.at[0]),
            fetch(intra.at[:, here], intra_v, sems.at[1]),
            fetch(gate.at[:, here], gate_v, sems.at[2]),
        ]
        load_weight = fetch(output_w, weight, sems.at[3])
        for load in loads:
            load.wait()
        for head in range(heads):
            span = slice(head * VAL_DIM, (head + 1) * VAL_DIM)
            q = wide(query_v[:, head * KEY_DIM : (head + 1) * KEY_DIM])
            scaled = low(q * decay_rows(decay[head], index * size + 1.0, size, 1.0))
            o = intra_v[span] + matmul_right(state[head], scaled)
            centred = o - jnp.mean(o, axis=0, keepdims=True)
            scale = lax.rsqrt(jnp.mean(centred * centred, axis=0, keepdims=True) + EPS)
            unit = centred * scale
            unit_v[span] = low(unit)
            scale_out[head] = jnp.broadcast_to(scale, (8, size))
            g = wide(gate_v[span])
            gated_v[span] = low(g * jax.nn.sigmoid(g) * unit)
        stores = [
            fetch(gated_v, gated.at[:, here], sems.at[4]),
            fetch(unit_v, units.at[:, here], sems.at[5]),
        ]
        load_weight.wait()
        part[...] = low(matmul_left(gated_v[...], weight[...]))
        for store in stores:
            store.wait()

    return pl.pallas_call(
        kernel,
        in_specs=[SMEM, ANY, ANY, ANY, VMEM, ANY] + [ANY] * (0 if first else 2),
        out_specs=[VMEM, VMEM, ANY, ANY],
        out_shape=[
            struct((size, width), jnp.bfloat16),
            in_hbm((heads, 8, size), jnp.float32),
            in_hbm((values, rows)),
            in_hbm((values, rows)),
        ],
        scratch_shapes=[
            vmem((size, keys)),
            vmem((values, size)),
            vmem((values, size), jnp.float32),
            vmem(output_w.shape),
            vmem((values, size)),
            vmem((values, size)),
            pltpu.SemaphoreType.DMA((6,)),
        ],
        input_output_aliases={} if first else {6: 2, 7: 3},
        compiler_params=params(20),
        cost_estimate=small_cost(),
    )(decay, pin(query), pin(gate), pin(intra), state, pin(output_w), *([] if first else map(pin, buffers)))


def feed_call(index, place, tok, gm, held, came, gain, bias, gate_w, up_w, down_w, buffers):
    rows, width = tok.shape
    size = held.shape[0]
    hidden = gate_w.shape[0]
    first = buffers is None

    def kernel(place, tok, gm, held, came, gain, bias, gate_w, up_w, down_w, *refs):
        refs = refs if first else refs[3:]
        part, small = refs[:2]
        mix_out, unit_out, scale_out, in_all, hidden_all, grads_all = refs[2:8]
        tok_v, gm_v, held_v, came_v, weights, down_v = refs[8:14]
        mix_v, unit_v, scale_v, in_v, hidden_v, grads_v, pre, grad_hidden, back, sums, sems = refs[14:]
        here = pl.ds(index * size, size)
        load_gm = fetch(gm.at[here], gm_v, sems.at[0])
        load_down = fetch(down_w, down_v, sems.at[1])
        inputs = [
            fetch(tok.at[here], tok_v, sems.at[2]),
            fetch(held, held_v, sems.at[3]),
            fetch(came, came_v, sems.at[4]),
        ]
        load_gate = fetch(gate_w, weights.at[pl.ds(0, hidden)], sems.at[5])
        load_up = fetch(up_w, weights.at[pl.ds(hidden, hidden)], sems.at[6])
        load_gm.wait()
        load_down.wait()
        grad_hidden[...] = matmul_right(down_v[...], gm_v[...])
        for load in inputs:
            load.wait()
        take = place[0] != 0

        def norm(span):
            mix = jnp.where(take, came_v[span], held_v[span])
            mix_v[span] = mix
            unit, _, scale = norm_parts(wide(tok_v[span]) + wide(mix))
            unit_v[span] = low(unit)
            scale_v[span] = spread_lanes(scale)
            in_v[span] = low(unit * gain[1:2] + bias[1:2])

        tiles(size, norm)
        stores = [
            fetch(mix_v, mix_out, sems.at[7]),
            fetch(unit_v, unit_out, sems.at[8]),
            fetch(scale_v, scale_out, sems.at[9]),
            fetch(in_v, in_all.at[here], sems.at[10]),
        ]
        load_gate.wait()
        load_up.wait()
        pre[...] = matmul_right(weights[...], in_v[...])
        slope, cubic = 0.7978845608028654, 0.044715

        def gate(span):
            other = pl.ds(span.start + hidden, span.size)
            u, w, gz = pre[span], pre[other], grad_hidden[span]
            square = u * u
            tanh = jnp.tanh(slope * u * (1.0 + cubic * square))
            half = 0.5 * (1.0 + tanh)
            gelu = u * half
            inner = slope * (1.0 + 3.0 * cubic * square)
            gelu_grad = half + 0.5 * u * (1.0 - tanh * tanh) * inner
            hidden_v[span] = low(gelu * w)
            grads_v[span] = low(gz * w * gelu_grad)
            grads_v[other] = low(gz * gelu)

        tiles(hidden, gate, 432)
        stores.append(fetch(hidden_v, hidden_all.at[:, here], sems.at[11]))
        stores.append(fetch(grads_v, grads_all.at[:, here], sems.at[12]))
        back[...] = matmul_left(grads_v[...], weights[...])
        sums[...] = jnp.zeros_like(sums)

        def finish(span):
            piece = back[span]
            part[span] = low(piece)
            scaled = piece * wide(unit_v[span])
            sums[0:1] = sums[0:1] + jnp.sum(scaled, axis=0, keepdims=True)
            sums[1:2] = sums[1:2] + jnp.sum(piece, axis=0, keepdims=True)

        tiles(size, finish)
        small[...] = sums[0:2]
        for store in stores:
            store.wait()

    chunk = (size, width)
    return pl.pallas_call(
        kernel,
        in_specs=[SMEM] + [ANY] * 4 + [VMEM] * 2 + [ANY] * 3 + [ANY] * (0 if first else 3),
        out_specs=[VMEM] * 2 + [ANY] * 6,
        out_shape=[
            struct(chunk, jnp.bfloat16),
            in_hbm((2, width), jnp.float32),
            in_hbm(chunk),
            in_hbm(chunk),
            in_hbm((size, 128), jnp.float32),
            in_hbm((rows, width)),
            in_hbm((hidden, rows)),
            in_hbm((2 * hidden, rows)),
        ],
        scratch_shapes=[vmem(chunk)] * 4
        + [
            vmem((2 * hidden, width)),
            vmem(down_w.shape),
            vmem(chunk),
            vmem(chunk),
            vmem((size, 128), jnp.float32),
            vmem(chunk),
            vmem((hidden, size)),
            vmem((2 * hidden, size)),
            vmem((2 * hidden, size), jnp.float32),
            vmem((hidden, size), jnp.float32),
            vmem(chunk, jnp.float32),
            vmem((8, width), jnp.float32),
            pltpu.SemaphoreType.DMA((13,)),
        ],
        input_output_aliases={} if first else {10 + i: 5 + i for i in range(3)},
        compiler_params=params(40),
        cost_estimate=small_cost(),
    )(place, pin(tok), pin(gm), held, came, gain, bias, pin(gate_w), pin(up_w), pin(down_w), *([] if first else map(pin, buffers)))


def down_call(hidden, down_w):
    tall, rows = hidden.shape
    width = down_w.shape[1]
    size = rows // CHUNKS

    def kernel(hidden, down_w, *refs):
        outs, (hidden_v, down_v, product, sems) = refs[:CHUNKS], refs[CHUNKS:]
        load_hidden = fetch(hidden, hidden_v, sems.at[0])
        load_down = fetch(down_w, down_v, sems.at[1])
        load_hidden.wait()
        load_down.wait()
        stores = []
        for half in range(2):
            span = slice(half * rows // 2, (half + 1) * rows // 2)
            product[span] = low(matmul_left(hidden_v[:, span], down_v[...]))
            for i in range(half * CHUNKS // 2, (half + 1) * CHUNKS // 2):
                piece = product.at[pl.ds(i * size, size)]
                stores.append(fetch(piece, outs[i], sems.at[2 + i]))
        for store in stores:
            store.wait()

    return pl.pallas_call(
        kernel,
        in_specs=[ANY, ANY],
        out_specs=[ANY] * CHUNKS,
        out_shape=[in_hbm((size, width))] * CHUNKS,
        scratch_shapes=[
            vmem(hidden.shape),
            vmem(down_w.shape),
            vmem((rows, width)),
            pltpu.SemaphoreType.DMA((2 + CHUNKS,)),
        ],
        compiler_params=params(32),
        cost_estimate=small_cost(),
    )(pin(hidden), pin(down_w))


def gate_call(index, place, decay, gm, held, came, gain, unit, scale, output_w, gate, units, scale_ret, query, total, buffers):
    rows, width = gm.shape
    size = held.shape[0]
    values = output_w.shape[0]
    heads = values // VAL_DIM
    keys = heads * KEY_DIM
    first, last = index == 0, index == CHUNKS - 1

    def kernel(place, decay, gm, held, came, gain, unit, scale, output_w, gate, units, scale_ret, query, *refs):
        if not first:
            total_in = refs[0]
            refs = refs[4:]
        total, grad_mid, mid_all, gate_all, ret_all = refs[:5]
        gm_v, held_v, came_v, unit_v, scale_v, weight, gate_v, units_v, query_v = refs[5:14]
        mid_v, low_v, grad_v, grads_gate, ret_v, sems = refs[14:]
        here = pl.ds(index * size, size)
        inputs = [
            fetch(gm.at[here], gm_v, sems.at[0]),
            fetch(held, held_v, sems.at[1]),
            fetch(came, came_v, sems.at[2]),
            fetch(unit, unit_v, sems.at[3]),
            fetch(scale, scale_v, sems.at[4]),
        ]
        load_weight = fetch(output_w, weight, sems.at[5])
        others = [
            fetch(gate.at[:, here], gate_v, sems.at[6]),
            fetch(units.at[:, here], units_v, sems.at[7]),
            fetch(query.at[here], query_v, sems.at[8]),
        ]
        for load in inputs:
            load.wait()
        take = place[0] != 0

        def norm(span):
            gc = wide(jnp.where(take, came_v[span], held_v[span])) * gain[1:2]
            mid = wide(gm_v[span]) + norm_back(gc, wide(unit_v[span]), scale_v[span][:, 0:1])
            mid_v[span] = mid
            low_v[span] = low(mid)

        tiles(size, norm)
        stores = [
            fetch(mid_v, grad_mid, sems.at[9]),
            fetch(low_v, mid_all.at[here], sems.at[10]),
        ]
        load_weight.wait()
        grad_v[...] = matmul_right(weight[...], low_v[...])
        for load in others:
            load.wait()
        for head in range(heads):
            span = pl.ds(head * VAL_DIM, VAL_DIM)
            gy, g, o = grad_v[span], wide(gate_v[span]), wide(units_v[span])
            s = jax.nn.sigmoid(g)
            grads_gate[span] = low(gy * o * (s * (1.0 + g * (1.0 - s))))
            grad = gy * (g * s)
            mean = jnp.mean(grad, axis=0, keepdims=True)
            along = jnp.mean(grad * o, axis=0, keepdims=True)
            ret_v[span] = low(scale_ret[head][0:1] * (grad - mean - o * along))
        stores.append(fetch(grads_gate, gate_all.at[:, here], sems.at[11]))
        stores.append(fetch(ret_v, ret_all.at[:, here], sems.at[12]))
        for head in range(heads):
            q = wide(query_v[:, head * KEY_DIM : (head + 1) * KEY_DIM])
            scaled = low(q * decay_rows(decay[head], index * size + 1.0, size, 1.0))
            own = matmul(ret_v[head * VAL_DIM : (head + 1) * VAL_DIM], scaled)
            if not first:
                own = own + total_in[head]
            total[head] = low(own) if last else own
        for store in stores:
            store.wait()

    chunk = (size, width)
    extra = [] if first else [total, *map(pin, buffers)]
    return pl.pallas_call(
        kernel,
        in_specs=[SMEM, SMEM, ANY, ANY, ANY, VMEM, ANY, ANY, ANY, ANY, ANY, VMEM, ANY]
        + ([] if first else [VMEM] + [ANY] * 3),
        out_specs=[VMEM] + [ANY] * 4,
        out_shape=[
            struct((heads, VAL_DIM, KEY_DIM), jnp.bfloat16 if last else jnp.float32),
            in_hbm(chunk, jnp.float32),
            in_hbm((rows, width)),
            in_hbm((values, rows)),
            in_hbm((values, rows)),
        ],
        scratch_shapes=[vmem(chunk)] * 4
        + [
            vmem((size, 128), jnp.float32),
            vmem(output_w.shape),
            vmem((values, size)),
            vmem((values, size)),
            vmem((size, keys)),
            vmem(chunk, jnp.float32),
            vmem(chunk),
            vmem((values, size), jnp.float32),
            vmem((values, size)),
            vmem((values, size)),
            pltpu.SemaphoreType.DMA((13,)),
        ],
        input_output_aliases={} if first else {14 + i: 2 + i for i in range(3)},
        compiler_params=params(28),
        cost_estimate=small_cost(),
    )(
        place,
        decay,
        pin(gm),
        held,
        came,
        gain,
        pin(unit),
        pin(scale),
        pin(output_w),
        pin(gate),
        pin(units),
        scale_ret,
        pin(query),
        *extra,
    )


def inner_call(decay, query, key, value, grad, state, cos, sin):
    rows, keys = query.shape
    heads = keys // KEY_DIM
    size = rows // CHUNKS

    def kernel(decay, query, key, value, grad, state, cos, sin, query_grad, key_part, value_part, weights, scores):
        span = lambda i: slice(i * size, (i + 1) * size)
        rate = decay[pl.program_id(0)]
        tables = [decay_square(rate, d * size, size) for d in range(CHUNKS)]
        for i in range(CHUNKS):
            q, go = query[span(i)], grad[:, span(i)]
            for j in range(i + 1):
                weights[span(i), span(j)] = low(matmul_right(q, key[span(j)]) * tables[i - j])
                scores[span(i), span(j)] = low(
                    matmul_left(go, value[:, span(j)]) * tables[i - j]
                )
            gq = decay_rows(rate, i * size + 1.0, size, 1.0) * matmul_left(go, state[0])
            gq = gq + matmul(scores[span(i), : (i + 1) * size], key[: (i + 1) * size])
            gq = turn(gq, cos[span(i)], -sin[span(i)]) * (1.0 / KEY_DIM**0.5)
            query_grad[span(i)] = low(gq)
        for j in range(CHUNKS):
            key_part[span(j)] = matmul_left(scores[j * size :, span(j)], query[j * size :])
            value_part[:, span(j)] = matmul(grad[:, j * size :], weights[j * size :, span(j)])

    column = pl.BlockSpec((rows, KEY_DIM), lambda h: (0, h))
    per_head = pl.BlockSpec((VAL_DIM, rows), lambda h: (h, 0))
    whole = lambda a: pl.BlockSpec(a.shape, lambda h: (0,) * a.ndim)
    return pl.pallas_call(
        kernel,
        grid=(heads,),
        in_specs=[
            SMEM,
            column,
            column,
            per_head,
            per_head,
            pl.BlockSpec((1, VAL_DIM, KEY_DIM), lambda h: (h, 0, 0)),
            whole(cos),
            whole(sin),
        ],
        out_specs=[column, column, per_head],
        out_shape=[
            in_hbm((rows, 2 * keys)),
            in_hbm((rows, keys), jnp.float32),
            in_hbm((heads * VAL_DIM, rows), jnp.float32),
        ],
        scratch_shapes=[vmem((rows, rows)), vmem((rows, rows))],
        compiler_params=params(44),
        cost_estimate=small_cost(),
    )(decay, pin(query), pin(key), pin(value), pin(grad), state, cos, sin)


def back_call(index, decay, tok, mean, scale, key, value, key_part, value_part, state, cos, sin, turned, gate_grad, weights, value_all, sums_before, sums_two):
    rows, width = tok.shape
    query_w, key_w, value_w, gate_w = weights
    keys, values = key_w.shape[1], value_w.shape[0]
    heads = keys // KEY_DIM
    size = 2 * rows // CHUNKS
    half = size // 2
    first = value_all is None
    last = size * (index + 1) == rows
    extra = EXTRA_ROWS if last else 0

    def kernel(decay, tok, mean, scale, key, value, key_part, value_part, state, cos, sin, gate_grad, query_w, key_w, value_w, gate_w, turned_in, *refs):
        refs = refs if first else refs[1:]
        before, refs = (refs[0], refs[1:]) if not first else (None, refs)
        two, refs = (refs[:CHUNKS], refs[CHUNKS:]) if last else ((), refs)
        part, other_part, small, turned_all, value_all = refs[:5]
        tok_v, mean_v, scale_v, key_v, value_v, key_p, value_p, turned_v, wide_v = refs[5:14]
        narrow_w, wide_w, total, sems = refs[14:]
        here = pl.ds(index * size, size)
        loads = [
            fetch(key_part.at[here], key_p, sems.at[0]),
            fetch(value_part.at[:, here], value_p, sems.at[1]),
            fetch(key.at[here], key_v, sems.at[2]),
            fetch(value.at[:, here], value_v, sems.at[3]),
        ]
        others = [
            fetch(turned_in.at[here, pl.ds(0, keys)], turned_v.at[:, pl.ds(0, keys)], sems.at[4]),
            fetch(gate_grad.at[:, here], wide_v.at[pl.ds(values, values)], sems.at[5]),
            fetch(query_w, narrow_w.at[:, pl.ds(0, keys)], sems.at[6]),
            fetch(key_w, narrow_w.at[:, pl.ds(keys, keys)], sems.at[7]),
            fetch(value_w, wide_w.at[pl.ds(0, values)], sems.at[8]),
            fetch(gate_w, wide_w.at[pl.ds(values, values)], sems.at[9]),
        ]
        norms = [
            fetch(tok.at[here], tok_v, sems.at[10]),
            fetch(mean.at[here], mean_v, sems.at[11]),
            fetch(scale.at[here], scale_v, sems.at[12]),
        ]
        for load in loads:
            load.wait()
        for head in range(heads):
            span = slice(head * KEY_DIM, (head + 1) * KEY_DIM)
            tall = slice(head * VAL_DIM, (head + 1) * VAL_DIM)
            scaling = decay_rows(decay[head], rows - 1.0 - index * size, size, -1.0)
            gk = key_p[:, span] + scaling * matmul_left(value_v[tall], state[head])
            turned_v[:, keys + span.start : keys + span.stop] = low(turn(gk, cos[...], -sin[...]))
            scaled = low(wide(key_v[:, span]) * scaling)
            wide_v[tall] = low(value_p[tall] + matmul_right(state[head], scaled))
        stores = [
            fetch(turned_v.at[:, pl.ds(keys, keys)], turned_all.at[here, pl.ds(keys, keys)], sems.at[13]),
            fetch(wide_v.at[pl.ds(0, values)], value_all.at[:, here], sems.at[14]),
        ]
        for load in others:
            load.wait()
        total[...] = matmul_right(turned_v[...], narrow_w[...]) + matmul_left(wide_v[...], wide_w[...])
        for load in norms:
            load.wait()
        gain, bias = jnp.zeros((1, width), jnp.float32), jnp.zeros((1, width), jnp.float32)
        if not first:
            gain, bias = before[0:1], before[1:2]
        for start in range(0, size, half):
            span = pl.ds(start, half)
            piece = total[span]
            if start:
                other_part[...] = low(piece)
            else:
                part[0:half] = low(piece)
            unit = (wide(tok_v[span]) - mean_v[span][:, 0:1]) * scale_v[span][:, 0:1]
            gain = gain + jnp.sum(piece * unit, axis=0, keepdims=True)
            bias = bias + jnp.sum(piece, axis=0, keepdims=True)
        small[0:1] = gain
        small[1:2] = bias
        if last:
            sums = sum(values[...] for values in two)
            fill = jnp.zeros((extra - 4, width), jnp.float32)
            part[half : half + extra] = low(jnp.concatenate([gain, bias, sums, fill], axis=0))
        for store in stores:
            store.wait()

    row = lambda cols: pl.BlockSpec((size, cols), lambda i: (index, 0))
    whole = lambda a: pl.BlockSpec(a.shape, lambda i: (0,) * len(a.shape))
    out_shape = [
        struct((half + extra, width), jnp.bfloat16),
        struct((half, width), jnp.bfloat16),
        struct((2, width), jnp.float32),
        in_hbm((rows, 2 * keys)),
        in_hbm((values, rows)),
    ]
    tail = [] if first else [pin(value_all), sums_before]
    tail += sums_two if last else []
    return pl.pallas_call(
        kernel,
        grid=(1,),
        in_specs=[SMEM]
        + [ANY] * 7
        + [whole(state), row(128), row(128)]
        + [ANY] * 6
        + ([] if first else [ANY, whole(sums_before)])
        + ([whole(sums_two[0])] * CHUNKS if last else []),
        out_specs=[whole(shape) for shape in out_shape[:3]] + [ANY, ANY],
        out_shape=out_shape,
        scratch_shapes=[
            vmem((size, width)),
            vmem((size, 128), jnp.float32),
            vmem((size, 128), jnp.float32),
            vmem((size, keys)),
            vmem((values, size)),
            vmem((size, keys), jnp.float32),
            vmem((values, size), jnp.float32),
            vmem((size, 2 * keys)),
            vmem((2 * values, size)),
            vmem((width, 2 * keys)),
            vmem((2 * values, width)),
            vmem((size, width), jnp.float32),
            pltpu.SemaphoreType.DMA((15,)),
        ],
        input_output_aliases={16: 3} if first else {16: 3, 17: 4},
        compiler_params=params(44),
        cost_estimate=small_cost(),
    )(
        decay,
        pin(tok),
        pin(mean),
        pin(scale),
        pin(key),
        pin(value),
        pin(key_part),
        pin(value_part),
        state,
        cos,
        sin,
        pin(gate_grad),
        *map(pin, weights),
        pin(turned),
        *tail,
    )


def tokens_call(index, place, held, came, tok, mean, scale, gain, grad_mid, out):
    rows, width = tok.shape
    size = rows // CHUNKS
    piece = size // 2

    def kernel(place, held, came, tok, mean, scale, gain, grad_mid, *refs):
        def body(span):
            ga = wide(jnp.where(place[0] != 0, came[span], held[span]))
            factor = scale[span][:, 0:1]
            unit = (wide(tok[span]) - mean[span][:, 0:1]) * factor
            refs[-1][span] = grad_mid[span] + norm_back(ga * gain[0:1], unit, factor)

        tiles(piece, body)

    row = lambda cols: pl.BlockSpec((piece, cols), lambda i: (2 * index + i, 0))
    chunk = pl.BlockSpec((piece, width), lambda i: (i, 0))
    first = out is None
    return pl.pallas_call(
        kernel,
        grid=(2,),
        in_specs=[SMEM, chunk, chunk, row(width), row(128), row(128)]
        + [pl.BlockSpec(gain.shape, lambda i: (0, 0)), chunk]
        + [ANY] * (not first),
        out_specs=row(width),
        out_shape=in_hbm((rows, width), jnp.float32),
        input_output_aliases={} if first else {8: 0},
        compiler_params=params(12),
        cost_estimate=small_cost(),
    )(place, held, came, pin(tok), pin(mean), pin(scale), gain, pin(grad_mid), *([] if first else [pin(out)]))


def result_call(index, place, held, came, tok, mix, out):
    rows, width = tok.shape
    size = held.shape[0]
    piece = size // 2

    def kernel(place, held, came, tok, mix, *refs):
        total = wide(jnp.where(place[0] != 0, came[...], held[...]))
        refs[-1][...] = low(wide(tok[...]) + wide(mix[...]) + total)

    row = pl.BlockSpec((piece, width), lambda i: (2 * index + i, 0))
    chunk = pl.BlockSpec((piece, width), lambda i: (i, 0))
    first = out is None
    return pl.pallas_call(
        kernel,
        grid=(2,),
        in_specs=[SMEM, chunk, chunk, row, chunk] + [ANY] * (not first),
        out_specs=row,
        out_shape=in_hbm((rows, width)),
        input_output_aliases={} if first else {5: 0},
        compiler_params=params(8),
        cost_estimate=small_cost(),
    )(place, held, came, pin(tok), pin(mix), *([] if first else [pin(out)]))


def product_call(pairs, tall):
    rows, cols = pairs[0][1].shape
    parts = 4
    block = cols // parts
    spans, at = [], 0
    for left, _ in pairs:
        spans.append((at, at + left.shape[0] // tall))
        at = spans[-1][1]

    def kernel(*refs):
        i = pl.program_id(0)
        for n, (begin, end) in enumerate(spans):

            @pl.when((i >= begin) & (i < end))
            def _():
                refs[-1][...] = low(matmul(refs[2 * n][...], refs[2 * n + 1][...]))

    specs = []
    for begin, end in spans:

        def left_map(i, j, begin=begin, end=end):
            return (jnp.clip(i - begin, 0, end - begin - 1), 0)

        def right_map(i, j, begin=begin, end=end):
            return (0, jnp.where(i < begin, 0, jnp.where(i < end, j, parts - 1)))

        specs += [pl.BlockSpec((tall, rows), left_map), pl.BlockSpec((rows, block), right_map)]

    return pl.pallas_call(
        kernel,
        grid=(at, parts),
        in_specs=specs,
        out_specs=pl.BlockSpec((tall, block), lambda i, j: (i, j)),
        out_shape=in_hbm((at * tall, cols)),
        compiler_params=params(36),
        cost_estimate=small_cost(),
    )(*[pin(values) for pair in pairs for values in pair])


def product_rows_call(left, right):
    rows, cols = left.shape
    wide_cols = right.shape[1]
    block = cols // 4

    def kernel(left, right, out):
        out[...] = low(matmul_left(left[...], right[...]))

    return pl.pallas_call(
        kernel,
        grid=(4,),
        in_specs=[
            pl.BlockSpec((rows, block), lambda j: (0, j)),
            pl.BlockSpec((rows, wide_cols), lambda j: (0, 0), pipeline_mode=pl.Buffered(1)),
        ],
        out_specs=pl.BlockSpec((block, wide_cols), lambda j: (j, 0)),
        out_shape=in_hbm((cols, wide_cols)),
        compiler_params=params(32),
        cost_estimate=small_cost(),
    )(pin(left), pin(right))


def combine_call(groups, axis, dtype, cuts=1):
    arrays = []
    for group in groups:
        for values, _, _ in group:
            if not any(values is a for a in arrays):
                arrays.append(values)
    runs = [
        [([a is values for a in arrays].index(True), start, stop) for values, start, stop in group]
        for group in groups
    ]
    long = sum(stop - start for _, start, stop in runs[0])
    shape = list(arrays[0].shape)
    shape[axis] = long
    piece = list(shape)
    piece[1 - axis] //= cuts
    count = sum(len(group) for group in runs)

    def along(ref, start, size):
        return ref.at[pl.ds(start, size)] if axis == 0 else ref.at[:, pl.ds(start, size)]

    def kernel(*refs):
        sources, outs = refs[: len(arrays)], refs[len(arrays) : len(arrays) + cuts]
        held, sems = refs[len(arrays) + cuts : -1], refs[-1]
        loads = []
        for group, target in zip(runs, held):
            at = 0
            for which, start, stop in group:
                source = along(sources[which], start, stop - start)
                copy = fetch(source, along(target, at, stop - start), sems.at[len(loads)])
                loads.append(copy)
                at += stop - start
        for load in loads:
            load.wait()
        total = wide(held[0][...])
        for values in held[1:]:
            total = total + wide(values[...])
        total = total.astype(dtype)
        for i, out in enumerate(outs):
            size = piece[1 - axis]
            out[...] = total[:, i * size : (i + 1) * size] if axis == 0 else total[i * size : (i + 1) * size]

    made = pl.pallas_call(
        kernel,
        in_specs=[ANY] * len(arrays),
        out_specs=[VMEM] * cuts,
        out_shape=[struct(piece, dtype)] * cuts,
        scratch_shapes=[vmem(shape)] * len(runs) + [pltpu.SemaphoreType.DMA((count,))],
        compiler_params=params(16),
        cost_estimate=small_cost(),
    )(*arrays)
    return made[0] if cuts == 1 else made


class Node:
    def __init__(self, fn, deps, cost, rank, link):
        self.fn, self.cost, self.rank, self.link = fn, cost, rank, link
        self.wanted = [dep if isinstance(dep, tuple) else (dep,) for dep in deps]
        self.deps = [dep[0] for dep in self.wanted]
        self.value = None
        self.ready = None
        self.after = []

    def given(self):
        return [
            {name: node.value[name] for name in names} if names else node.value
            for node, *names in self.wanted
        ]


class Plan:
    def __init__(self):
        self.nodes = []

    def work(self, fn, deps, cost, rank):
        self.nodes.append(Node(fn, deps, cost, rank, None))
        return self.nodes[-1]

    def move(self, fn, deps, cost, link, rank=0):
        self.nodes.append(Node(fn, deps, cost, rank, link))
        return self.nodes[-1]

    def run(self):
        now, token, free, flying = 0.0, None, {}, []
        left = list(self.nodes)
        while left:
            known = [n for n in left if all(d.ready is not None for d in n.deps + n.after)]
            views = [n for n in known if n.link == "view"]
            moves = [n for n in known if n.link not in (None, "view")]
            able = [n for n in known if n.link is None]
            calls = [n for n in moves if n.link in CALLS]
            moves = [
                n
                for n in sorted(moves, key=lambda n: n.rank)
                if n.link not in CALLS
                and free.get(n.link, 0.0) - now <= QUEUE_TIME
                and len(flying) < FLYING
            ]
            fresh = all(now - f.issued <= FRESH_TIME or f.rank == SLACK for f in flying)
            if calls and (fresh and not moves or not (able or moves)):
                moves = calls
            if views or moves:
                node = (views or moves)[0]
                given = node.given()
                if token is not None and (node.link != "view" or len(given) > 1):
                    given, _ = lax.optimization_barrier((given, token))
                node.value = node.fn(*given)
                node.ready = max(d.ready for d in node.deps)
                left.remove(node)
                if node.link != "view":
                    node.ready = max(node.ready, now, free.get(node.link, 0.0)) + node.cost
                    free[node.link] = node.ready
                    now += START_COST
                    node.issued = now
                    if node.link not in CALLS:
                        flying.append(node)
                continue
            if not able:
                now += 1.0
                continue
            when = {id(n): max([d.ready for d in n.deps] + [0.0]) for n in able}
            oldest = {}
            for n in able:
                started = [d.issued for d in n.deps if d in flying]
                oldest[id(n)] = min(started) if started else None
            at_hand = [n for n in able if when[id(n)] <= now]
            arrived = [n for n in at_hand if oldest[id(n)] is not None]
            if arrived:
                next_in_order = min(arrived, key=lambda n: oldest[id(n)])
                at_hand = [n for n in at_hand if n not in arrived or n is next_in_order]
            if at_hand:
                node = min(at_hand, key=lambda n: n.rank)
            else:
                soon = [when[id(n)] for n in able]
                waiting = [
                    free[n.link] - QUEUE_TIME
                    for n in known
                    if n.link in free and n.link not in CALLS and free[n.link] - now > QUEUE_TIME
                ]
                if waiting and min(waiting) < min(soon, default=1e9) and len(flying) < FLYING:
                    now = min(waiting)
                    continue
                node = min(able, key=lambda n: (when[id(n)], n.rank))
                now = when[id(node)]
            given = node.given()
            if token is not None:
                given, _ = lax.optimization_barrier((given, token))
            made = lax.optimization_barrier(node.fn(*given))
            leaves = jax.tree.leaves(made)
            token = min(leaves, key=lambda leaf: leaf.size)
            node.value = made
            now += node.cost
            node.ready = now
            left.remove(node)
            flying = [f for f in flying if f not in node.deps]


FLYING = 5
FRESH_TIME = 14.0
SLACK = 1.5
QUEUE_TIME = 6.0
CALLS = ("scatter", "gather")
START_COST = 2.0
LINK_RATE = 100e3
CORE_RATE = 300e3


def head_total(plan, part, size, rank):
    count = lax.axis_size("head")
    mid = count // 2
    cost = size * 2 / LINK_RATE + 1.5

    def permute(pairs):
        return lambda held: lax.ppermute(held, "head", pairs)

    held = part
    for step in range(mid - 1):
        pairs = [(step, step + 1), (count - 1 - step, count - 2 - step)]
        came = plan.move(permute(pairs), [held], cost, ("in", step), rank)
        held = plan.work(add_call, [held, came], 1.5, rank)
    came = plan.move(permute([(mid - 1, mid), (mid, mid - 1)]), [held], cost, "swap", rank)
    held = plan.work(add_call, [held, came], 1.5, rank)
    for step in range(mid - 1):
        pairs = [(mid - 1 - step, mid - 2 - step), (mid + step, mid + 1 + step)]
        came = plan.move(permute(pairs), [held], cost, ("out", step), rank)
        if step < mid - 2:
            held = plan.work(out_pick(step), [held, came], 2.0, rank)
    return [held, came] if mid > 1 else [held, held]


def out_pick(step):
    def pick(held, came):
        place = lax.axis_index("head")
        mid = lax.axis_size("head") // 2
        return jnp.where((place == mid - 2 - step) | (place == mid + 1 + step), came, held)

    return pick


def exchange(values, bit):
    count = lax.axis_size("seq")
    return lax.ppermute(values, "seq", [(i, i ^ bit) for i in range(count)])


def seq_bits(flip):
    count = lax.axis_size("seq")
    bits = [1 << i for i in range(count.bit_length() - 1)]
    return [bits[0]] + bits[:0:-1] if flip else bits


def halving_lists(bits, count):
    kept = [0]
    levels = []
    for bit in reversed(bits):
        sent = [block ^ bit for block in kept]
        levels.append((bit, sent))
        kept = sent + kept
    levels.reverse()
    return levels


def arrangement(count):
    bits = [1 << i for i in range(count.bit_length() - 1)]
    if count == 8:
        kept = [2, 6, 4, 0]
        return [block ^ 1 for block in kept] + kept
    order = [0]
    for bit in reversed(bits):
        order = [block ^ bit for block in order] + order
    return order


def grad_scatter(plan, arranged, other, shape, flip, rows_last, limit, rank, cuts=1):
    count = lax.axis_size("seq")
    axis = 1 if rows_last else 0
    width = shape[axis] // count
    size = shape[0] * shape[1] * 2

    def whole(values, right):
        if rows_last:
            return product_call([(right, values)], right.shape[0])
        return product_rows_call(values, right)

    def runs_of(parts, lists, wanted):
        runs = []
        for block in wanted:
            array, at = next(
                (a, blocks.index(block)) for a, blocks in zip(parts, lists) if block in blocks
            )
            if runs and runs[-1][0] is array and runs[-1][2] == at * width:
                runs[-1] = (array, runs[-1][1], (at + 1) * width)
            else:
                runs.append((array, at * width, (at + 1) * width))
        return runs

    def level(wanted, groups, last):
        def fn(*parts):
            taken, at = [], 0
            for lists in groups:
                taken.append(runs_of(parts[at : at + len(lists)], lists, wanted))
                at += len(lists)
            return combine_call(taken, axis, jnp.float32 if last else jnp.bfloat16, cuts if last else 1)

        return fn

    made = plan.work(whole, [arranged, other], size / 2 * 2 * 1024 / 750e6 + 1.0, rank)
    groups, parts = [[arrangement(count)]], [made]
    for bit, sent in halving_lists(seq_bits(flip), count):
        pieces = 2 if size * len(sent) / count > limit else 1
        lists = []
        for piece in range(pieces):
            blocks = sent[len(sent) * piece // pieces : len(sent) * (piece + 1) // pieces]
            share = size * len(blocks) / count
            given = plan.work(
                level(blocks, list(groups), False), list(parts), share / 0.8e6 + 0.7, rank
            )
            came = plan.move(
                lambda v, bit=bit: exchange(v, bit),
                [given],
                2.0 + (share / CORE_RATE if bit == 1 else share * 2 / LINK_RATE),
                ("seq", bit),
                rank,
            )
            lists.append((came, [block ^ bit for block in blocks]))
        groups.append([blocks for _, blocks in lists])
        parts += [came for came, _ in lists]
    return plan.work(level([0], list(groups), True), list(parts), 2.0, rank)


def small_total(plan, values, rank):
    def halves(bit, keep):
        def fn(values, *came):
            half = values.shape[1] // 2
            high = ((lax.axis_index("seq") & bit) != 0) == keep
            part = jnp.where(high, values[:, half:], values[:, :half])
            return part + came[0] if came else part

        return fn

    bit = lax.axis_size("seq") // 2
    while bit:
        sent = plan.work(halves(bit, False), [values], 0.7, rank)
        came = plan.move(lambda v, bit=bit: exchange(v, bit), [sent], 3.5, ("seq", bit), rank)
        values = plan.work(halves(bit, True), [values, came], 0.7, rank)
        bit //= 2
    return values


def scan_states(plan, own, shape, log_decay, rows, backward, rank):
    count = lax.axis_size("seq")
    size = shape[0] * shape[1] * shape[2] * 2

    def update(group, last):
        def fn(total, came, *before):
            place = lax.axis_index("seq")
            inside = place & (group - 1)
            later = (place & group) != 0
            if backward:
                inside = group - 1 - inside
                later = ~later
            power = lambda n: jnp.exp(n * rows * log_decay)[:, None, None]
            mine, other = wide(total), wide(came)
            state = jnp.where(later, other * power(wide(inside)), 0.0)
            if before:
                state = state + before[0]
            if last:
                return low(state)
            spread = power(float(group))
            joined = jnp.where(later, other * spread + mine, mine * spread + other)
            return dict(total=low(joined), state=state)

        return fn

    total, state, group = own, [], 1
    while group < count:
        link = ("seq", group)
        time = 2.0 + (size / CORE_RATE if group == 1 else size * 2 / LINK_RATE)
        came = plan.move(lambda v, group=group: exchange(v, group), [total], time, link, rank)
        last = group * 2 == count
        node = plan.work(update(group, last), [total, came] + state, 1.5, rank)
        if last:
            return node
        total = plan.move(lambda v: v["total"], [(node, "total")], 0.0, "view")
        state = [plan.move(lambda v: v["state"], [(node, "state")], 0.0, "view")]
        group *= 2


def rotation(rows):
    half = KEY_DIM // 2
    positions = wide(lax.axis_index("seq") * rows + jnp.arange(rows, dtype=jnp.int32))
    freqs = 1.0 / 10000.0 ** jnp.linspace(0.0, 1.0, half, dtype=jnp.float32)
    angles = positions[:, None] * freqs[None, :]
    return jnp.cos(angles), jnp.sin(angles)


FED = ("in_all", "hidden_all", "grads_all")
BACK = ("total", "grad_mid", "mid_all", "gate_all", "ret_all")
MIX = ("gated", "units")


def on_device(
    tokens,
    norm_gain,
    norm_bias,
    query_weight,
    key_weight,
    value_weight,
    gate_weight,
    output_weight,
    ffn_gate,
    ffn_up,
    ffn_down,
    grad_out,
):
    rows, width = tokens.shape
    query_w, key_w, value_w, gate_w = (
        query_weight[0],
        key_weight[0],
        value_weight[0].T,
        gate_weight[0].T,
    )
    output_w, ffn_gate_w, ffn_up_w, ffn_down_w = (
        output_weight[0],
        ffn_gate[0].T,
        ffn_up[0].T,
        ffn_down[0],
    )
    gains, biases = norm_gain[0], norm_bias[0]
    heads_here = query_w.shape[1] // KEY_DIM
    keys_here = query_w.shape[1]
    values_here = value_w.shape[0]
    hidden_here = ffn_gate_w.shape[0]
    step = rows // CHUNKS
    count = lax.axis_size("seq")
    ends = lax.axis_index("head")
    ends = (ends == 0) | (ends == lax.axis_size("head") - 1)

    head_ids = wide(lax.axis_index("head") * heads_here) + jnp.arange(heads_here, dtype=jnp.float32)
    log_decay = jnp.log1p(-jnp.exp2(-5.0 - head_ids))
    cosine, sine = rotation(rows)
    order = arrangement(count)
    relative = jnp.bitwise_xor(
        jnp.arange(count, dtype=jnp.int32), lax.axis_index("seq").astype(jnp.int32)
    )
    position = sum(jnp.where(relative == block, order.index(block), 0) for block in order)
    place = jnp.concatenate([ends.astype(jnp.int32)[None], position.astype(jnp.int32)])

    plan = Plan()

    def view(fn, *deps):
        return plan.move(fn, list(deps), 0.0, "view")

    def pick(name, node, *after):
        return view(lambda v, *_: v[name], (node, name), *[(n, name) for n in after])

    def start(tokens):
        names = ("normed", "mean", "scale", "key", "value", "own_state")
        made = first_call(log_decay, tokens, gains, biases, cosine, sine, key_w, value_w)
        return dict(zip(names, made))

    def queries(first):
        made = second_call(place, first["normed"], cosine, sine, query_w, gate_w)
        return dict(zip(("query", "gate", "arranged"), made))

    def within(first, second):
        return intra_call(log_decay, second["query"], first["key"], first["value"])

    given, grad_given = Node(None, [], 0.0, 0, None), Node(None, [], 0.0, 0, None)
    given.value, given.ready = tokens, 0.0
    grad_given.value, grad_given.ready = grad_out, 0.0
    first = plan.work(start, [given], 13.0, 0)
    state_shape = (heads_here, VAL_DIM, KEY_DIM)
    state = scan_states(
        plan, pick("own_state", first), state_shape, log_decay, rows, False, 0
    )
    second = plan.work(queries, [(first, "normed")], 12.0, 1)
    intra = plan.work(within, [(first, "key", "value"), (second, "query")], 10.0, 2)

    def mix(index):
        def fn(second, intra, state, *before):
            made = mix_call(
                index,
                log_decay,
                second["query"],
                second["gate"],
                intra,
                state,
                output_w,
                [before[0][name] for name in MIX] if before else None,
            )
            return dict(zip(("part", "scale_ret") + MIX, made))

        return fn

    def feed(index):
        def fn(held, came, *before):
            buffers = [before[0][name] for name in FED] if before else None
            made = feed_call(
                index,
                place,
                tokens,
                grad_out,
                held,
                came,
                gains,
                biases,
                ffn_gate_w,
                ffn_up_w,
                ffn_down_w,
                buffers,
            )
            return dict(zip(("part", "small", "mix", "unit", "scale") + FED, made))

        return fn

    def back_gate(index):
        def fn(fed, mixed, units, second, held, came, *before):
            total = before[0]["total"] if before else None
            buffers = [before[0][name] for name in BACK[2:]] if before else None
            made = gate_call(
                index,
                place,
                log_decay,
                grad_out,
                held,
                came,
                gains,
                fed["unit"],
                fed["scale"],
                output_w,
                second["gate"],
                units["units"],
                mixed["scale_ret"],
                second["query"],
                total,
                buffers,
            )
            return dict(zip(BACK, made))

        return fn

    chunk_bytes = step * width * 2
    mixed, fed, back, outcome, grad_tokens, outer = [], [], [], [], [], []
    for index in range(CHUNKS):
        mixed.append(plan.work(mix(index), [(second, "query", "gate"), intra, state] + [(m, *MIX) for m in mixed[-1:]], 5.0, 0))
    for index in range(CHUNKS):
        total = head_total(plan, pick("part", mixed[index]), chunk_bytes, 1)
        fed.append(plan.work(feed(index), total + [(f, *FED) for f in fed[-1:]], 13.5, 2))
    for index in range(CHUNKS):
        total = head_total(plan, pick("part", fed[index]), chunk_bytes, 1)
        back.append(
            plan.work(
                back_gate(index),
                [
                    (fed[index], "unit", "scale"),
                    (mixed[index], "scale_ret"),
                    (mixed[-1], "units"),
                    (second, "gate", "query"),
                    *total,
                    *[(b, "total", *BACK[2:]) for b in back[-1:]],
                ],
                7.0,
                3,
            )
        )

    def result(index):
        def fn(fed, held, came, *before):
            return result_call(
                index, place, held, came, tokens, fed["mix"], before[0] if before else None
            )

        return fn

    def inside(first, second, state, back):
        made = inner_call(
            log_decay,
            second["query"],
            first["key"],
            first["value"],
            back["ret_all"],
            state,
            cosine,
            sine,
        )
        return dict(zip(("turned", "key_part", "value_part"), made))

    inner = plan.work(inside, [(first, "key", "value"), (second, "query"), state, (back[-1], "ret_all")], 9.0, 2.9)
    grad_state = scan_states(
        plan, pick("total", back[-1]), state_shape, log_decay, rows, True, 2.9
    )

    def keys_values(index):
        def fn(first, inner, grad_state, last, *others):
            before = others[0] if index else None
            made = back_call(
                index,
                log_decay,
                tokens,
                first["mean"],
                first["scale"],
                first["key"],
                first["value"],
                inner["key_part"],
                inner["value_part"],
                grad_state,
                cosine,
                sine,
                before["turned"] if before else inner["turned"],
                last["gate_all"],
                (query_w, key_w, value_w, gate_w),
                before["value_grad"] if before else None,
                before["small"] if before else None,
                [other["small"] for other in others[1:]],
            )
            return dict(zip(("part", "other_part", "small", "turned", "value_grad"), made))

        return fn

    def tokens_grad(index):
        def fn(first, back, held, came, *before):
            return tokens_call(
                index,
                place,
                held,
                came,
                tokens,
                first["mean"],
                first["scale"],
                gains,
                back["grad_mid"],
                before[0] if before else None,
            )

        return fn

    for index in range(CHUNKS // 2):
        outer.append(
            plan.work(
                keys_values(index),
                [
                    (first, "mean", "scale", "key", "value"),
                    (inner, "key_part", "value_part") + (() if outer else ("turned",)),
                    grad_state,
                    (back[-1], "gate_all"),
                    *[(o, "turned", "value_grad", "small") for o in outer[-1:]],
                    *([(f, "small") for f in fed] if index == CHUNKS // 2 - 1 else []),
                ],
                15.3,
                2.8,
            )
        )
    small = None
    for index in range(CHUNKS):
        name = "other_part" if index % 2 else "part"
        total = head_total(plan, pick(name, outer[index // 2]), chunk_bytes, 1)
        if index == CHUNKS - 2:
            small = total
        grad_tokens.append(
            plan.work(
                tokens_grad(index),
                [(first, "mean", "scale"), (back[index], "grad_mid")] + total + grad_tokens[-1:],
                4.1,
                5,
            )
        )

    def stacked(pairs, tall, rank):
        blocks = sum(count for _, _, count in pairs)
        fn = lambda *v: product_call(list(zip(v[0::2], v[1::2])), tall)
        deps = [node for left, right, _ in pairs for node in (left, right)]
        return plan.work(fn, deps, blocks * tall * width * 2 / 0.6e6 + 1.0, rank)

    called = []

    def scattered(made, tall, blocks):
        done = plan.move(
            lambda v: lax.psum_scatter(v, "seq", scatter_dimension=1, tiled=True),
            [made],
            tall * blocks * width * 2 / 73e3,
            "scatter",
        )
        called.append(done)
        split = lambda v: combine_call([[(v, 0, v.shape[1])]], 1, jnp.float32, blocks)
        return plan.work(split, [done], 1.0 + blocks, 30)

    arranged = pick("arranged", second)
    ffn_products = stacked(
        [
            (pick("grads_all", fed[-1]), pick("in_all", fed[-1]), 2),
            (pick("hidden_all", fed[-1]), grad_given, 1),
        ],
        hidden_here,
        2.95,
    )
    grads_ffn = scattered(ffn_products, hidden_here, 3)
    mix_products = stacked(
        [
            (pick("gated", mixed[-1]), pick("mid_all", back[-1]), 1),
            (pick("gate_all", back[-1]), pick("normed", first), 1),
        ],
        values_here,
        2.97,
    )
    grads_mix = scattered(mix_products, values_here, 2)

    down_parts = plan.work(
        lambda hidden: down_call(hidden, ffn_down_w),
        [pick("hidden_all", fed[-1])],
        9.0,
        2.965,
    )
    for index in range(CHUNKS):
        part = view(lambda v, index=index: v[index], down_parts)
        part.after = called[:1]
        total = head_total(plan, part, chunk_bytes, 1.5)
        outcome.append(plan.work(
                result(index), [(fed[index], "mix")] + total + outcome[-1:], 2.7, 3.3
            ))

    grad_turned = grad_scatter(
        plan, arranged, pick("turned", outer[-1]), (width, 2 * keys_here), False, False, chunk_bytes, 4.5, 2
    )
    grad_value_w = grad_scatter(
        plan, arranged, pick("value_grad", outer[-1]), (values_here, width), True, True, chunk_bytes, 4.6
    )
    def norm_sums(held, came):
        rows_small = jnp.where(ends, came, held) if lax.axis_size("head") > 2 else held
        return wide(rows_small[step : step + 4])

    small = small_total(plan, plan.work(norm_sums, small, 1.0, 4.8), 4.8)
    plan.run()
    small = small.value
    return (
        outcome[-1].value,
        grad_tokens[-1].value,
        small[0::2][None],
        small[1::2][None],
        grad_turned.value[0][None],
        grad_turned.value[1][None],
        grad_value_w.value.T[None],
        grads_mix.value[1].T[None],
        grads_mix.value[0][None],
        grads_ffn.value[0].T[None],
        grads_ffn.value[1].T[None],
        grads_ffn.value[2][None],
    )


def solution(mesh):
    return jax.shard_map(
        on_device,
        mesh=mesh,
        in_specs=(
            P("seq", None),
            P(),
            P(),
            P(None, None, "head"),
            P(None, None, "head"),
            P(None, None, "head"),
            P(None, None, "head"),
            P(None, "head", None),
            P(None, None, "head"),
            P(None, None, "head"),
            P(None, "head", None),
            P("seq", None),
        ),
        out_specs=(
            P("seq", None),
            P("seq", None),
            P(None, None, "seq"),
            P(None, None, "seq"),
            P(None, "seq", "head"),
            P(None, "seq", "head"),
            P(None, "seq", "head"),
            P(None, "seq", "head"),
            P(None, "head", "seq"),
            P(None, "seq", "head"),
            P(None, "seq", "head"),
            P(None, "head", "seq"),
        ),
        check_vma=False,
    )
```
